32 devices in a mesh: blk: 4 (over x, core), grp: 8 (over z, y).
Axes of the slice: x: 2, y: 2, z: 4, core: 2. Of those that a mesh axis runs over, the one named last changes fastest.
Arguments:
- features: float32 [4, 8, 4, 64, 1024], P('blk', 'grp'), may hold values from -6 to 6
- inv_scale: float32 [64], replicated, may hold values from 0.01 to 0.2
- solution: float32 [4, 8, 4, 16, 1024], P('blk', 'grp'), may hold values from -6 to 6
- residual: float32 [4, 8, 4, 16, 1024], P('blk', 'grp'), may hold values from -6 to 6
- direction: float32 [4, 8, 4, 16, 1024], P('blk', 'grp'), may hold values from -6 to 6
- neighbours: int32 [4, 8, 4, 8], P('blk', 'grp'), may hold values from 0 to 127, as said below
Outputs:
- new_solution: float32 [4, 8, 4, 16, 1024], P('blk', 'grp')
- new_residual: float32 [4, 8, 4, 16, 1024], P('blk', 'grp')
- new_direction: float32 [4, 8, 4, 16, 1024], P('blk', 'grp')
The draws below stay inside these ranges and needn't reach their ends.
Inputs may be any that keep to these rules, and one draw needn't show every extreme that they name: `neighbours`: each tile's list holds 8 different tile ids, among them the tile's own. The tile k of the device at blk b, grp g has id (b * 8 + g) * 4 + k. Listed tiles lie on the tile's own device, on the devices one step either way along blk (the blk index taken modulo 4), or on the devices one step either way along grp (no wrap).
All inputs are finite; a program needn't handle non-finite values.
Results may differ from the reference program's by a relative error of at most 0.00015.
Values sent between devices are 32-bit elements; how exact they have to be, the bound alone decides.
A program may use at most 64 MiB of HBM per device.

```python
import math
import jax
import jax.numpy as jnp
from jax import lax

F = 64
NVEC = 16
TILE = 1024
NEIGH = 8
TILES_DEV = 4
BLOCKS = 4
MEMBERS = 8


def draw_neighbours(key, part):
    key = jax.random.fold_in(key, 7)
    cand_count = 5 * TILES_DEV
    blk_ids = jnp.arange(BLOCKS, dtype=jnp.int32)[:, None, None, None]
    grp_ids = jnp.arange(MEMBERS, dtype=jnp.int32)[None, :, None, None]
    own_tile = jnp.arange(TILES_DEV, dtype=jnp.int32)[None, None, :, None]
    slot_ids = jnp.arange(cand_count, dtype=jnp.int32)[None, None, None, :]
    source = slot_ids // TILES_DEV
    within = slot_ids % TILES_DEV
    shift_blk = jnp.where(source == 1, BLOCKS - 1, jnp.where(source == 2, 1, 0))
    shift_grp = jnp.where(source == 3, -1, jnp.where(source == 4, 1, 0))
    far_blk = (blk_ids + shift_blk) % BLOCKS
    far_grp = grp_ids + shift_grp
    usable = (far_grp >= 0) & (far_grp < MEMBERS)
    tile_ids = (far_blk * MEMBERS + far_grp) * TILES_DEV + within
    shape = (BLOCKS, MEMBERS, TILES_DEV, cand_count)
    scores = jax.random.randint(key, shape, 0, 1 << 20, dtype=jnp.int32) * 128 + slot_ids
    scores = jnp.where(slot_ids == own_tile, 1 << 30, scores)
    scores = jnp.where(usable, scores, -1)
    _, picked = lax.top_k(scores, NEIGH)
    tile_ids = jnp.broadcast_to(tile_ids, shape).astype(jnp.int32)
    return jnp.take_along_axis(tile_ids, picked.astype(jnp.int32), axis=3).astype(jnp.int32)


def steps_of(stream_key, shape, pieces, low, high):
    loudness = 1.0
    for position, blocks in pieces:
        steps = jax.random.uniform(jax.random.fold_in(jax.random.fold_in(stream_key, 6), position), (blocks,), jnp.float32, low / len(pieces), high / len(pieces))
        loudness = loudness * jnp.repeat(jnp.exp(steps), shape[position] // blocks).reshape((-1,) + (1,) * (len(shape) - 1 - position))
    return loudness


def noise(stream_key, shape, width, limit, cuts=(), kind=jnp.bfloat16):
    factor_of = steps_of(stream_key, shape, cuts, -0.22, 0.18) if cuts else 1.0
    entries = jax.random.normal(stream_key, shape, jnp.float32) * width * factor_of
    return jnp.minimum(jnp.maximum(entries, -limit), limit).astype(kind)


def setup_inputs(seed: int = 0) -> dict:
    key_of = jax.random.split(jax.random.key(seed), 7)
    return {
        "features": noise(key_of[0], (BLOCKS, MEMBERS, TILES_DEV, F, TILE), 1.0, 6.0, ((0, 4), (1, 8)), jnp.float32),
        "inv_scale": jnp.clip(jnp.exp(jax.random.uniform(key_of[1], (F,), jnp.float32, math.log(0.01), math.log(0.2))), 0.01, 0.2),
        "solution": noise(key_of[2], (BLOCKS, MEMBERS, TILES_DEV, NVEC, TILE), 1.0, 6.0, ((0, 4), (1, 8)), jnp.float32),
        "residual": noise(key_of[3], (BLOCKS, MEMBERS, TILES_DEV, NVEC, TILE), 1.0, 6.0, ((0, 4), (1, 8)), jnp.float32),
        "direction": noise(key_of[4], (BLOCKS, MEMBERS, TILES_DEV, NVEC, TILE), 1.0, 6.0, ((0, 4), (1, 8)), jnp.float32),
        "neighbours": draw_neighbours(jax.random.fold_in(key_of[6], 71), 0),
    }


NOISE = 0.5

def wendland_terms(column_x, column_vec, row_x, row_norm):
    column_norm = lax.optimization_barrier(jnp.sum(column_x * column_x, axis=0))
    crossed = jnp.einsum('fr,ft->rt', column_x, row_x, precision=lax.Precision.HIGHEST, preferred_element_type=jnp.float32)
    squared = column_norm[:, None] + row_norm[None, :] - 2.0 * crossed
    radius = jnp.sqrt(jnp.maximum(squared, 0.0))
    remain = jnp.maximum(1.0 - radius, 0.0)
    weights = remain * remain * remain * remain * (4.0 * radius + 1.0)
    return jnp.dot(column_vec, weights, precision=lax.Precision.HIGHEST, preferred_element_type=jnp.float32)

def reference(features, inv_scale, solution, residual, direction, neighbours):
    tile_count = BLOCKS * MEMBERS * TILES_DEV
    scaled = (features * inv_scale[:, None]).reshape(tile_count, F, TILE)
    tile_dirs = direction.reshape(tile_count, NVEC, TILE)
    tile_lists = neighbours.reshape(tile_count, NEIGH).astype(jnp.int32)

    def one_tile(inputs_row):
        row_x, slot_ids = inputs_row
        row_norm = lax.optimization_barrier(jnp.sum(row_x * row_x, axis=0))

        def accumulate(running, slot_id):
            return (running + wendland_terms(scaled[slot_id], tile_dirs[slot_id], row_x, row_norm), None)
        running, _ = lax.scan(accumulate, jnp.zeros((NVEC, TILE), jnp.float32), slot_ids)
        return running
    product = (lax.map(one_tile, (scaled, tile_lists)) + NOISE * tile_dirs).reshape(direction.shape)
    axes_all = (0, 1, 2, 4)
    start_norm = lax.optimization_barrier(jnp.sum(residual * residual, axis=axes_all))
    curvature = lax.optimization_barrier(jnp.sum(direction * product, axis=axes_all))
    step_size = (start_norm / curvature)[:, None]
    new_solution = solution + step_size * direction
    new_residual = residual - step_size * product
    fresh_norm = lax.optimization_barrier(jnp.sum(new_residual * new_residual, axis=axes_all))
    new_direction = new_residual + (fresh_norm / start_norm)[:, None] * direction
    return (new_solution, new_residual, new_direction)
```

```python
import functools

import jax
import jax.numpy as jnp
from jax import lax
from jax.experimental import pallas as pl
from jax.experimental.pallas import tpu as pltpu
from jax.sharding import PartitionSpec as P

NOISE = 0.5
ROWS = 256
COLS = 256
LIMIT = 48 * 1024 * 1024
MESH = pl.DeviceIdType.MESH


def split_two(value):
    high = value.astype(jnp.bfloat16).astype(jnp.float32)
    return high, value - high


def split_norm(norm):
    first, rest = split_two(norm)
    second, third = split_two(rest)
    return [first, second, third]


def operand_rows(points, is_row):
    high, low = split_two(points)
    low = low.astype(jnp.bfloat16).astype(jnp.float32)
    feat = points.shape[0]
    kept = feat - 8
    norm = 16.0 * jnp.sum(high * (high + 2.0 * low), axis=0, keepdims=True)
    norm = norm + 16.0 * jnp.sum(low[:kept] * low[:kept], axis=0, keepdims=True)
    parts = split_norm(norm)
    shape = (8, points.shape[1])
    place = lax.broadcasted_iota(jnp.int32, shape, 0)
    first = 0 if is_row else 3
    tail = jnp.where(place < 6, 1.0, 0.0)
    for k in range(3):
        tail = jnp.where(place == first + k, jnp.broadcast_to(parts[k], shape), tail)
    if is_row:
        scaled_high, scaled_low = -32.0 * high, -32.0 * low
        return jnp.concatenate([scaled_high, scaled_high, scaled_low, scaled_low[:kept], tail], axis=0)
    return jnp.concatenate([high, low, high, low[:kept], tail], axis=0)


def vector_rows(vectors):
    high, low = split_two(vectors * (1.0 / 256.0))
    return jnp.concatenate([high, low], axis=0).astype(jnp.bfloat16)


def add_pair(row_ref, col_ref, vec_ref, acc_ref, s, t):
    tile = col_ref.shape[2]

    def one_block(step, _):
        rows = pl.ds(pl.multiple_of(step * ROWS, ROWS), ROWS)
        left = row_ref[s, rows, :]
        total = acc_ref[s, rows, :]
        for start in range(0, tile, COLS):
            squared = jnp.dot(left, col_ref[t, :, start : start + COLS], preferred_element_type=jnp.float32)
            squared = jnp.maximum(squared, 1e-30)
            radius = squared * lax.rsqrt(squared)
            remain = jnp.maximum(4.0 - radius, 0.0)
            square = remain * remain
            weight = (square * square) * (5.0 - remain)
            high = weight.astype(jnp.bfloat16)
            low = (weight - high.astype(jnp.float32)).astype(jnp.bfloat16)
            vec = vec_ref[t, :, start : start + COLS]
            dims = (((1,), (1,)), ((), ()))
            total = total + lax.dot_general(high, vec, dims, preferred_element_type=jnp.float32)
            total = total + lax.dot_general(low, vec, dims, preferred_element_type=jnp.float32)
        acc_ref[s, rows, :] = total
        return 0

    lax.fori_loop(0, tile // ROWS, one_block, 0)


def place_of(tile_id, tiles_here):
    blk_count, grp_count = lax.axis_size("blk"), lax.axis_size("grp")
    device = lax.div(tile_id, tiles_here)
    within = lax.rem(tile_id, tiles_here)
    step_blk = lax.rem(lax.div(device, grp_count) - lax.axis_index("blk") + blk_count, blk_count)
    step_grp = lax.rem(device, grp_count) - lax.axis_index("grp")
    return step_blk, step_grp, within


def walk(ids_ref, slot_of, row_ref, col_ref, vec_ref, acc_ref):
    tiles_here, listed = ids_ref.shape

    def visit(index, _):
        s = lax.div(index, listed)
        n = lax.rem(index, listed)
        slot = slot_of(*place_of(ids_ref[s, n], tiles_here))

        @pl.when(slot >= 0)
        def _():
            add_pair(row_ref, col_ref, vec_ref, acc_ref, s, slot)

        return 0

    lax.fori_loop(0, tiles_here * listed, visit, 0)


def folded(acc_ref, k, nvec):
    turned = acc_ref[k].T
    return turned[:nvec] + turned[nvec:]


def own_kernel(feat, ids_ref, packed_ref, row_ref, part_ref, col_ref, vec_ref, acc_ref):
    tiles = packed_ref.shape[0]
    nvec = packed_ref.shape[1] - feat
    for k in range(tiles):
        points = packed_ref[k, :feat]
        row_ref[k] = operand_rows(points, True).T.astype(jnp.bfloat16)
        col_ref[k] = operand_rows(points, False).astype(jnp.bfloat16)
        vec_ref[k] = vector_rows(packed_ref[k, feat:])
    acc_ref[...] = jnp.zeros_like(acc_ref)

    def slot_of(step_blk, step_grp, within):
        return jnp.where((step_blk == 0) & (step_grp == 0), within, -1)

    walk(ids_ref, slot_of, row_ref, col_ref, vec_ref, acc_ref)
    for k in range(tiles):
        part_ref[k] = NOISE * packed_ref[k, feat:] + folded(acc_ref, k, nvec)


def side_kernel(feat, along_blk, ids_ref, prior_ref, next_ref, row_ref, before_ref, part_ref, col_ref, vec_ref, acc_ref):
    tiles = prior_ref.shape[0]
    nvec = prior_ref.shape[1] - feat
    for source, ref in enumerate((prior_ref, next_ref)):
        for k in range(tiles):
            col_ref[source * tiles + k] = operand_rows(ref[k, :feat], False).astype(jnp.bfloat16)
            vec_ref[source * tiles + k] = vector_rows(ref[k, feat:])
    acc_ref[...] = jnp.zeros_like(acc_ref)

    def slot_of(step_blk, step_grp, within):
        if along_blk:
            return jnp.where(step_blk == 0, -1, jnp.where(step_blk == 1, tiles + within, within))
        side = jnp.where(step_grp < 0, within, tiles + within)
        return jnp.where((step_blk == 0) & (step_grp != 0), side, -1)

    walk(ids_ref, slot_of, row_ref, col_ref, vec_ref, acc_ref)
    for k in range(tiles):
        part_ref[k] = before_ref[k] + folded(acc_ref, k, nvec)


def scratch(cols, feat, nvec, tiles, tile):
    return [
        pltpu.VMEM((cols, 4 * feat, tile), jnp.bfloat16),
        pltpu.VMEM((cols, 2 * nvec, tile), jnp.bfloat16),
        pltpu.VMEM((tiles, tile, 2 * nvec), jnp.float32),
    ]


def cost(pairs, tile):
    return pl.CostEstimate(flops=int(pairs * tile * tile * 2048), bytes_accessed=4 << 20, transcendentals=0)


def in_smem():
    return pl.BlockSpec(memory_space=pltpu.SMEM)


def in_vmem():
    return pl.BlockSpec(memory_space=pltpu.VMEM)


def own_pairs(ids, packed, feat):
    tiles, width, tile = packed.shape
    nvec = width - feat
    return pl.pallas_call(
        functools.partial(own_kernel, feat),
        out_shape=(
            jax.ShapeDtypeStruct((tiles, tile, 4 * feat), jnp.bfloat16),
            jax.ShapeDtypeStruct((tiles, nvec, tile), jnp.float32),
        ),
        in_specs=[in_smem(), in_vmem()],
        out_specs=(in_vmem(), in_vmem()),
        scratch_shapes=scratch(tiles, feat, nvec, tiles, tile),
        compiler_params=pltpu.CompilerParams(vmem_limit_bytes=LIMIT),
        cost_estimate=cost(8, tile),
        name="own_pairs",
    )(ids, packed)


def side_pairs(ids, prior, following, rows, before, feat, along_blk):
    tiles, width, tile = prior.shape
    nvec = width - feat
    return pl.pallas_call(
        functools.partial(side_kernel, feat, along_blk),
        out_shape=jax.ShapeDtypeStruct((tiles, nvec, tile), jnp.float32),
        in_specs=[in_smem()] + [in_vmem()] * 4,
        out_specs=in_vmem(),
        scratch_shapes=scratch(2 * tiles, feat, nvec, tiles, tile),
        compiler_params=pltpu.CompilerParams(vmem_limit_bytes=LIMIT),
        cost_estimate=cost(12, tile),
        name="blk_pairs" if along_blk else "grp_pairs",
    )(ids, prior, following, rows, before)


def sums_kernel(part_ref, residual_ref, direction_ref, out_ref, held_ref, blk_ref, grp_ref, send_sem, blk_sem, grp_sem):
    blk_count, grp_count = lax.axis_size("blk"), lax.axis_size("grp")
    blk_index, grp_index = lax.axis_index("blk"), lax.axis_index("grp")
    barrier = pltpu.get_barrier_semaphore()

    def blk_partner(k):
        return (lax.rem(blk_index + k, blk_count), grp_index)

    def grp_partner(k):
        return (blk_index, lax.rem(grp_index + k, grp_count))

    def greet(partner, k, _):
        pl.semaphore_signal(barrier, inc=1, device_id=partner(k), device_id_type=MESH)
        return 0

    lax.fori_loop(1, blk_count, functools.partial(greet, blk_partner), 0)
    lax.fori_loop(1, grp_count, functools.partial(greet, grp_partner), 0)

    nvec = part_ref.shape[1]
    lane = lax.broadcasted_iota(jnp.int32, (nvec, 128), 1)

    def total_of(first_ref, second_ref):
        both = jnp.sum(first_ref[...] * second_ref[...], axis=0)
        return jnp.sum(both, axis=1, keepdims=True)

    held = jnp.zeros((nvec, 128), jnp.float32)
    pairs = (
        (residual_ref, residual_ref),
        (direction_ref, part_ref),
        (residual_ref, part_ref),
        (part_ref, part_ref),
    )
    for k, (first_ref, second_ref) in enumerate(pairs):
        held = jnp.where(lane == k, total_of(first_ref, second_ref), held)
    held_ref[0] = held
    pl.semaphore_wait(barrier, blk_count + grp_count - 2)

    def swap(source, landing, sems, partner, count):
        def copy_of(k):
            return pltpu.make_async_remote_copy(
                src_ref=source,
                dst_ref=landing.at[k],
                send_sem=send_sem.at[k],
                recv_sem=sems.at[k],
                device_id=partner(k),
                device_id_type=MESH,
            )

        def begin(k, _):
            copy_of(k).start()
            return 0

        def end(k, _):
            copy_of(k).wait()
            return 0

        lax.fori_loop(1, count, begin, 0)
        lax.fori_loop(1, count, end, 0)

        def add(k, total):
            return total + landing[k]

        return lax.fori_loop(1, count, add, source[...])

    held_ref[1] = swap(held_ref.at[0], blk_ref, blk_sem, blk_partner, blk_count)
    out_ref[...] = swap(held_ref.at[1], grp_ref, grp_sem, grp_partner, grp_count)


def summed(part, residual, direction):
    nvec = part.shape[1]
    blk_count, grp_count = lax.axis_size("blk"), lax.axis_size("grp")
    return pl.pallas_call(
        sums_kernel,
        out_shape=jax.ShapeDtypeStruct((nvec, 128), jnp.float32),
        in_specs=[in_vmem()] * 3,
        out_specs=in_vmem(),
        scratch_shapes=[
            pltpu.VMEM((2, nvec, 128), jnp.float32),
            pltpu.VMEM((blk_count, nvec, 128), jnp.float32),
            pltpu.VMEM((grp_count, nvec, 128), jnp.float32),
            pltpu.SemaphoreType.DMA((max(blk_count, grp_count),)),
            pltpu.SemaphoreType.DMA((blk_count,)),
            pltpu.SemaphoreType.DMA((grp_count,)),
        ],
        compiler_params=pltpu.CompilerParams(collective_id=0, has_side_effects=True),
        name="sums",
    )(part, residual, direction)


def per_device(features, inv_scale, solution, residual, direction, neighbours):
    feat = features.shape[3]
    blk_count, grp_count = lax.axis_size("blk"), lax.axis_size("grp")
    packed = jnp.concatenate([features[0, 0] * inv_scale[:, None], direction[0, 0]], axis=1)
    ids = neighbours[0, 0]
    up = [(i, (i + 1) % blk_count) for i in range(blk_count)]
    down = [((i + 1) % blk_count, i) for i in range(blk_count)]
    prior_blk = lax.ppermute(packed, "blk", up)
    next_blk = lax.ppermute(packed, "blk", down)
    prior_grp = lax.ppermute(packed, "grp", [(i, i + 1) for i in range(grp_count - 1)])
    next_grp = lax.ppermute(packed, "grp", [(i + 1, i) for i in range(grp_count - 1)])
    rows, part = own_pairs(ids, packed, feat)
    part = side_pairs(ids, prior_blk, next_blk, rows, part, feat, True)
    part = side_pairs(ids, prior_grp, next_grp, rows, part, feat, False)
    sums = summed(part, residual[0, 0], direction[0, 0])
    start_norm, curvature, crossed, length = (sums[:, k : k + 1] for k in range(4))
    step = start_norm / curvature
    fresh_norm = jnp.maximum(start_norm + step * (step * length - 2.0 * crossed), 0.0)
    new_residual = residual - step * part
    new_solution = solution + step * direction
    new_direction = new_residual + (fresh_norm / start_norm) * direction
    return (new_solution, new_residual, new_direction)


def solution(mesh):
    split = P("blk", "grp", None, None, None)
    in_specs = (split, P(), split, split, split, P("blk", "grp", None, None))
    return jax.shard_map(per_device, mesh=mesh, in_specs=in_specs, out_specs=(split, split, split), check_vma=False)
```

```python
import functools

import jax
import jax.numpy as jnp
from jax import lax
from jax.experimental import pallas as pl
from jax.experimental.pallas import tpu as pltpu
from jax.sharding import PartitionSpec as P

NOISE = 0.5
ROWS = 512
COLS = 256
LIMIT = 48 * 1024 * 1024
MESH = pl.DeviceIdType.MESH


def split_two(value):
    high = value.astype(jnp.bfloat16).astype(jnp.float32)
    return high, value - high


def split_norm(norm):
    first, rest = split_two(norm)
    second, third = split_two(rest)
    return [first, second, third]


def operand_rows(points, is_row):
    high, low = split_two(points)
    low = low.astype(jnp.bfloat16).astype(jnp.float32)
    feat = points.shape[0]
    kept = feat - 8
    norm = 16.0 * jnp.sum(high * (high + 2.0 * low), axis=0, keepdims=True)
    norm = norm + 16.0 * jnp.sum(low[:kept] * low[:kept], axis=0, keepdims=True)
    parts = split_norm(norm)
    shape = (8, points.shape[1])
    place = lax.broadcasted_iota(jnp.int32, shape, 0)
    first = 0 if is_row else 3
    tail = jnp.where(place < 6, 1.0, 0.0)
    for k in range(3):
        tail = jnp.where(place == first + k, jnp.broadcast_to(parts[k], shape), tail)
    if is_row:
        scaled_high, scaled_low = -32.0 * high, -32.0 * low
        return jnp.concatenate([scaled_high, scaled_high, scaled_low, scaled_low[:kept], tail], axis=0)
    return jnp.concatenate([high, low, high, low[:kept], tail], axis=0)


def vector_rows(vectors):
    high, low = split_two(vectors * (1.0 / 256.0))
    return jnp.concatenate([high, low], axis=0).astype(jnp.bfloat16)


def add_pair(row_ref, col_ref, vec_ref, acc_ref, s, t):
    depth, tile = row_ref.shape[1:]
    places = [(r, c) for c in range(0, tile, COLS) for r in range(0, tile, ROWS)]

    def squared_of(place):
        r, c = place
        return jnp.dot(col_ref[t, r : r + ROWS, :], row_ref[s, :, c : c + COLS], preferred_element_type=jnp.float32)

    ahead = squared_of(places[0])
    for k, (r, c) in enumerate(places):
        squared = jnp.maximum(ahead, 1e-30)
        if k + 1 < len(places):
            ahead = squared_of(places[k + 1])
        radius = squared * lax.rsqrt(squared)
        remain = jnp.maximum(4.0 - radius, 0.0)
        square = remain * remain
        weight = (square * square) * (5.0 - remain)
        high = weight.astype(jnp.bfloat16)
        low = (weight - high.astype(jnp.float32)).astype(jnp.bfloat16)
        vec = vec_ref[t, :, r : r + ROWS]
        acc_ref[s, :, c : c + COLS] += jnp.dot(
            jnp.concatenate([vec, vec], axis=1),
            jnp.concatenate([high, low], axis=0),
            preferred_element_type=jnp.float32,
        )


def place_of(tile_id, tiles_here):
    blk_count, grp_count = lax.axis_size("blk"), lax.axis_size("grp")
    device = lax.div(tile_id, tiles_here)
    within = lax.rem(tile_id, tiles_here)
    step_blk = lax.rem(lax.div(device, grp_count) - lax.axis_index("blk") + blk_count, blk_count)
    step_grp = lax.rem(device, grp_count) - lax.axis_index("grp")
    return step_blk, step_grp, within


def walk(ids_ref, slot_of, row_ref, col_ref, vec_ref, acc_ref):
    tiles_here, listed = ids_ref.shape

    def visit(index, _):
        s = lax.div(index, listed)
        n = lax.rem(index, listed)
        slot = slot_of(*place_of(ids_ref[s, n], tiles_here))

        @pl.when(slot >= 0)
        def _():
            add_pair(row_ref, col_ref, vec_ref, acc_ref, s, slot)

        return 0

    lax.fori_loop(0, tiles_here * listed, visit, 0)


def folded(acc_ref, k, nvec):
    return acc_ref[k, :nvec] + acc_ref[k, nvec:]


def own_kernel(feat, ids_ref, packed_ref, row_ref, part_ref, col_ref, vec_ref, acc_ref):
    tiles = packed_ref.shape[0]
    nvec = packed_ref.shape[1] - feat
    for k in range(tiles):
        points = packed_ref[k, :feat]
        row_ref[k] = operand_rows(points, True).astype(jnp.bfloat16)
        col_ref[k] = operand_rows(points, False).astype(jnp.bfloat16).T
        vec_ref[k] = vector_rows(packed_ref[k, feat:])
    acc_ref[...] = jnp.zeros_like(acc_ref)

    def slot_of(step_blk, step_grp, within):
        return jnp.where((step_blk == 0) & (step_grp == 0), within, -1)

    walk(ids_ref, slot_of, row_ref, col_ref, vec_ref, acc_ref)
    for k in range(tiles):
        part_ref[k] = NOISE * packed_ref[k, feat:] + folded(acc_ref, k, nvec)


def side_kernel(feat, along_blk, ids_ref, prior_ref, next_ref, row_ref, before_ref, part_ref, col_ref, vec_ref, acc_ref):
    tiles = prior_ref.shape[0]
    nvec = prior_ref.shape[1] - feat
    for source, ref in enumerate((prior_ref, next_ref)):
        for k in range(tiles):
            col_ref[source * tiles + k] = operand_rows(ref[k, :feat], False).astype(jnp.bfloat16).T
            vec_ref[source * tiles + k] = vector_rows(ref[k, feat:])
    acc_ref[...] = jnp.zeros_like(acc_ref)

    def slot_of(step_blk, step_grp, within):
        if along_blk:
            return jnp.where(step_blk == 0, -1, jnp.where(step_blk == 1, tiles + within, within))
        side = jnp.where(step_grp < 0, within, tiles + within)
        return jnp.where((step_blk == 0) & (step_grp != 0), side, -1)

    walk(ids_ref, slot_of, row_ref, col_ref, vec_ref, acc_ref)
    for k in range(tiles):
        part_ref[k] = before_ref[k] + folded(acc_ref, k, nvec)


def scratch(cols, feat, nvec, tiles, tile):
    return [
        pltpu.VMEM((cols, tile, 4 * feat), jnp.bfloat16),
        pltpu.VMEM((cols, 2 * nvec, tile), jnp.bfloat16),
        pltpu.VMEM((tiles, 2 * nvec, tile), jnp.float32),
    ]


def cost(pairs, tile):
    return pl.CostEstimate(flops=int(pairs * tile * tile * 2048), bytes_accessed=4 << 20, transcendentals=0)


def in_smem():
    return pl.BlockSpec(memory_space=pltpu.SMEM)


def in_vmem():
    return pl.BlockSpec(memory_space=pltpu.VMEM)


def own_pairs(ids, packed, feat):
    tiles, width, tile = packed.shape
    nvec = width - feat
    return pl.pallas_call(
        functools.partial(own_kernel, feat),
        out_shape=(
            jax.ShapeDtypeStruct((tiles, 4 * feat, tile), jnp.bfloat16),
            jax.ShapeDtypeStruct((tiles, nvec, tile), jnp.float32),
        ),
        in_specs=[in_smem(), in_vmem()],
        out_specs=(in_vmem(), in_vmem()),
        scratch_shapes=scratch(tiles, feat, nvec, tiles, tile),
        compiler_params=pltpu.CompilerParams(vmem_limit_bytes=LIMIT),
        cost_estimate=cost(8, tile),
        name="own_pairs",
    )(ids, packed)


def side_pairs(ids, prior, following, rows, before, feat, along_blk):
    tiles, width, tile = prior.shape
    nvec = width - feat
    return pl.pallas_call(
        functools.partial(side_kernel, feat, along_blk),
        out_shape=jax.ShapeDtypeStruct((tiles, nvec, tile), jnp.float32),
        in_specs=[in_smem()] + [in_vmem()] * 4,
        out_specs=in_vmem(),
        scratch_shapes=scratch(2 * tiles, feat, nvec, tiles, tile),
        compiler_params=pltpu.CompilerParams(vmem_limit_bytes=LIMIT),
        cost_estimate=cost(12, tile),
        name="blk_pairs" if along_blk else "grp_pairs",
    )(ids, prior, following, rows, before)


def sums_kernel(part_ref, residual_ref, direction_ref, out_ref, held_ref, blk_ref, grp_ref, send_sem, blk_sem, grp_sem):
    blk_count, grp_count = lax.axis_size("blk"), lax.axis_size("grp")
    blk_index, grp_index = lax.axis_index("blk"), lax.axis_index("grp")
    barrier = pltpu.get_barrier_semaphore()

    def blk_partner(k):
        return (lax.rem(blk_index + k, blk_count), grp_index)

    def grp_partner(k):
        return (blk_index, lax.rem(grp_index + k, grp_count))

    def greet(partner, k, _):
        pl.semaphore_signal(barrier, inc=1, device_id=partner(k), device_id_type=MESH)
        return 0

    lax.fori_loop(1, blk_count, functools.partial(greet, blk_partner), 0)
    lax.fori_loop(1, grp_count, functools.partial(greet, grp_partner), 0)

    nvec = part_ref.shape[1]
    lane = lax.broadcasted_iota(jnp.int32, (nvec, 128), 1)

    def total_of(first_ref, second_ref):
        both = jnp.sum(first_ref[...] * second_ref[...], axis=0)
        return jnp.sum(both, axis=1, keepdims=True)

    held = jnp.zeros((nvec, 128), jnp.float32)
    pairs = (
        (residual_ref, residual_ref),
        (direction_ref, part_ref),
        (residual_ref, part_ref),
        (part_ref, part_ref),
    )
    for k, (first_ref, second_ref) in enumerate(pairs):
        held = jnp.where(lane == k, total_of(first_ref, second_ref), held)
    held_ref[0] = held
    pl.semaphore_wait(barrier, blk_count + grp_count - 2)

    def swap(source, landing, sems, partner, count):
        def copy_of(k):
            return pltpu.make_async_remote_copy(
                src_ref=source,
                dst_ref=landing.at[k],
                send_sem=send_sem.at[k],
                recv_sem=sems.at[k],
                device_id=partner(k),
                device_id_type=MESH,
            )

        def begin(k, _):
            copy_of(k).start()
            return 0

        def end(k, _):
            copy_of(k).wait()
            return 0

        lax.fori_loop(1, count, begin, 0)
        lax.fori_loop(1, count, end, 0)

        def add(k, total):
            return total + landing[k]

        return lax.fori_loop(1, count, add, source[...])

    held_ref[1] = swap(held_ref.at[0], blk_ref, blk_sem, blk_partner, blk_count)
    sums = swap(held_ref.at[1], grp_ref, grp_sem, grp_partner, grp_count)
    start_norm, curvature, crossed, length = (sums[:, k : k + 1] for k in range(4))
    step = start_norm / curvature
    fresh_norm = jnp.maximum(start_norm + step * (step * length - 2.0 * crossed), 0.0)
    out_ref[...] = jnp.where(lane == 0, step, fresh_norm / start_norm)


def summed(part, residual, direction):
    nvec = part.shape[1]
    blk_count, grp_count = lax.axis_size("blk"), lax.axis_size("grp")
    return pl.pallas_call(
        sums_kernel,
        out_shape=jax.ShapeDtypeStruct((nvec, 128), jnp.float32),
        in_specs=[in_vmem()] * 3,
        out_specs=in_vmem(),
        scratch_shapes=[
            pltpu.VMEM((2, nvec, 128), jnp.float32),
            pltpu.VMEM((blk_count, nvec, 128), jnp.float32),
            pltpu.VMEM((grp_count, nvec, 128), jnp.float32),
            pltpu.SemaphoreType.DMA((max(blk_count, grp_count),)),
            pltpu.SemaphoreType.DMA((blk_count,)),
            pltpu.SemaphoreType.DMA((grp_count,)),
        ],
        compiler_params=pltpu.CompilerParams(collective_id=0, has_side_effects=True),
        name="sums",
    )(part, residual, direction)


def per_device(features, inv_scale, solution, residual, direction, neighbours):
    feat = features.shape[3]
    blk_count, grp_count = lax.axis_size("blk"), lax.axis_size("grp")
    packed = jnp.concatenate([features[0, 0] * inv_scale[:, None], direction[0, 0]], axis=1)
    ids = neighbours[0, 0]
    up = [(i, (i + 1) % blk_count) for i in range(blk_count)]
    down = [((i + 1) % blk_count, i) for i in range(blk_count)]
    prior_blk = lax.ppermute(packed, "blk", up)
    next_blk = lax.ppermute(packed, "blk", down)
    prior_grp = lax.ppermute(packed, "grp", [(i, i + 1) for i in range(grp_count - 1)])
    next_grp = lax.ppermute(packed, "grp", [(i + 1, i) for i in range(grp_count - 1)])
    rows, part = own_pairs(ids, packed, feat)
    part = side_pairs(ids, prior_blk, next_blk, rows, part, feat, True)
    part = side_pairs(ids, prior_grp, next_grp, rows, part, feat, False)
    factors = summed(part, residual[0, 0], direction[0, 0])
    step, ratio = factors[:, :1], factors[:, 1:2]
    new_residual = residual - step * part
    new_solution = solution + step * direction
    new_direction = new_residual + ratio * direction
    return (new_solution, new_residual, new_direction)


def solution(mesh):
    split = P("blk", "grp", None, None, None)
    in_specs = (split, P(), split, split, split, P("blk", "grp", None, None))
    return jax.shard_map(per_device, mesh=mesh, in_specs=in_specs, out_specs=(split, split, split), check_vma=False)
```

```python
import functools

import jax
import jax.numpy as jnp
from jax import lax
from jax.experimental import pallas as pl
from jax.experimental.pallas import tpu as pltpu
from jax.sharding import PartitionSpec as P

NOISE = 0.5
ROWS = 512
COLS = 256
LIMIT = 24 * 1024 * 1024
MESH = pl.DeviceIdType.MESH


def split_two(value):
    high = value.astype(jnp.bfloat16).astype(jnp.float32)
    return high, value - high


def split_norm(norm):
    first, rest = split_two(norm)
    second, third = split_two(rest)
    return [first, second, third]


def operand_rows(points, is_row):
    high, low = split_two(points)
    low = low.astype(jnp.bfloat16).astype(jnp.float32)
    feat = points.shape[0]
    kept = feat - 8
    norm = 16.0 * jnp.sum(high * (high + 2.0 * low), axis=0, keepdims=True)
    norm = norm + 16.0 * jnp.sum(low[:kept] * low[:kept], axis=0, keepdims=True)
    parts = split_norm(norm)
    shape = (8, points.shape[1])
    place = lax.broadcasted_iota(jnp.int32, shape, 0)
    first = 0 if is_row else 3
    tail = jnp.where(place < 6, 1.0, 0.0)
    for k in range(3):
        tail = jnp.where(place == first + k, jnp.broadcast_to(parts[k], shape), tail)
    if is_row:
        scaled_high, scaled_low = -32.0 * high, -32.0 * low
        return jnp.concatenate([scaled_high, scaled_high, scaled_low, scaled_low[:kept], tail], axis=0)
    return jnp.concatenate([high, low, high, low[:kept], tail], axis=0)


def vector_rows(vectors):
    high, low = split_two(vectors * (1.0 / 256.0))
    return jnp.concatenate([high, low], axis=0).astype(jnp.bfloat16)


def add_pair(row_ref, col_ref, vec_ref, acc_ref, s, t):
    depth, tile = row_ref.shape[1:]
    places = [(r, c) for c in range(0, tile, COLS) for r in range(0, tile, ROWS)]

    def squared_of(place):
        r, c = place
        return jnp.dot(col_ref[t, r : r + ROWS, :], row_ref[s, :, c : c + COLS], preferred_element_type=jnp.float32)

    ahead = squared_of(places[0])
    for k, (r, c) in enumerate(places):
        squared = jnp.maximum(ahead, 1e-30)
        if k + 1 < len(places):
            ahead = squared_of(places[k + 1])
        radius = squared * lax.rsqrt(squared)
        remain = jnp.maximum(4.0 - radius, 0.0)
        square = remain * remain
        weight = (square * square) * (5.0 - remain)
        high = weight.astype(jnp.bfloat16)
        low = (weight - high.astype(jnp.float32)).astype(jnp.bfloat16)
        vec = vec_ref[t, :, r : r + ROWS]
        acc_ref[s, :, c : c + COLS] += jnp.dot(
            jnp.concatenate([vec, vec], axis=1),
            jnp.concatenate([high, low], axis=0),
            preferred_element_type=jnp.float32,
        )


def place_of(tile_id, tiles_here):
    blk_count, grp_count = lax.axis_size("blk"), lax.axis_size("grp")
    device = lax.div(tile_id, tiles_here)
    within = lax.rem(tile_id, tiles_here)
    step_blk = lax.rem(lax.div(device, grp_count) - lax.axis_index("blk") + blk_count, blk_count)
    step_grp = lax.rem(device, grp_count) - lax.axis_index("grp")
    return step_blk, step_grp, within


def walk(ids_ref, slot_of, row_ref, col_ref, vec_ref, acc_ref):
    tiles_here, listed = ids_ref.shape

    def visit(index, _):
        s = lax.div(index, listed)
        n = lax.rem(index, listed)
        slot = slot_of(*place_of(ids_ref[s, n], tiles_here))

        @pl.when(slot >= 0)
        def _():
            add_pair(row_ref, col_ref, vec_ref, acc_ref, s, slot)

        return 0

    lax.fori_loop(0, tiles_here * listed, visit, 0)


def folded(acc_ref, k, nvec):
    return acc_ref[k, :nvec] + acc_ref[k, nvec:]


def own_kernel(feat, ids_ref, packed_ref, row_ref, part_ref, col_ref, vec_ref, acc_ref):
    tiles = packed_ref.shape[0]
    nvec = packed_ref.shape[1] - feat
    for k in range(tiles):
        points = packed_ref[k, :feat]
        row_ref[k] = operand_rows(points, True).astype(jnp.bfloat16)
        col_ref[k] = operand_rows(points, False).astype(jnp.bfloat16).T
        vec_ref[k] = vector_rows(packed_ref[k, feat:])
    acc_ref[...] = jnp.zeros_like(acc_ref)

    def slot_of(step_blk, step_grp, within):
        return jnp.where((step_blk == 0) & (step_grp == 0), within, -1)

    walk(ids_ref, slot_of, row_ref, col_ref, vec_ref, acc_ref)
    for k in range(tiles):
        part_ref[k] = NOISE * packed_ref[k, feat:] + folded(acc_ref, k, nvec)


def build_columns(sources, feat, col_ref, vec_ref):
    for k, (ref, tile) in enumerate(sources):
        col_ref[k] = operand_rows(ref[tile, :feat], False).astype(jnp.bfloat16).T
        vec_ref[k] = vector_rows(ref[tile, feat:])


def near_step():
    return 1 - 2 * lax.rem(lax.axis_index("grp"), 2)


def mid_kernel(feat, ids_ref, prior_ref, next_ref, near_ref, row_ref, before_ref, part_ref, col_ref, vec_ref, acc_ref):
    tiles = prior_ref.shape[0]
    nvec = prior_ref.shape[1] - feat
    build_columns([(ref, k) for ref in (prior_ref, next_ref, near_ref) for k in range(tiles)], feat, col_ref, vec_ref)
    acc_ref[...] = jnp.zeros_like(acc_ref)

    def slot_of(step_blk, step_grp, within):
        beside = jnp.where(step_grp == near_step(), 2 * tiles + within, -1)
        return jnp.where(step_blk == 0, beside, jnp.where(step_blk == 1, tiles + within, within))

    walk(ids_ref, slot_of, row_ref, col_ref, vec_ref, acc_ref)
    for k in range(tiles):
        part_ref[k] = before_ref[k] + folded(acc_ref, k, nvec)


def far_kernel(
    feat, ids_ref, far_ref, row_ref, before_ref, residual_ref, direction_ref, part_ref, sums_ref, col_ref, vec_ref, acc_ref
):
    tiles = far_ref.shape[0]
    nvec = far_ref.shape[1] - feat
    build_columns([(far_ref, k) for k in range(tiles)], feat, col_ref, vec_ref)
    acc_ref[...] = jnp.zeros_like(acc_ref)

    def slot_of(step_blk, step_grp, within):
        return jnp.where((step_blk == 0) & (step_grp == -near_step()), within, -1)

    walk(ids_ref, slot_of, row_ref, col_ref, vec_ref, acc_ref)
    for k in range(tiles):
        part_ref[k] = before_ref[k] + folded(acc_ref, k, nvec)
    lane = lax.broadcasted_iota(jnp.int32, (nvec, 128), 1)
    part, residual, direction = part_ref[...], residual_ref[...], direction_ref[...]
    held = jnp.zeros((nvec, 128), jnp.float32)
    for k, both in enumerate((residual * residual, direction * part, residual * part, part * part)):
        total = jnp.sum(jnp.sum(both, axis=0), axis=1, keepdims=True)
        held = jnp.where(lane == k, total, held)
    sums_ref[...] = held


def update_kernel(factors_ref, part_ref, solution_ref, residual_ref, direction_ref, x_ref, r_ref, d_ref):
    step, ratio = factors_ref[:, :1], factors_ref[:, 1:2]
    for k in range(part_ref.shape[0]):
        direction = direction_ref[k]
        residual = residual_ref[k] - step * part_ref[k]
        x_ref[k] = solution_ref[k] + step * direction
        r_ref[k] = residual
        d_ref[k] = residual + ratio * direction


def scratch(cols, feat, nvec, tiles, tile):
    return [
        pltpu.VMEM((cols, tile, 4 * feat), jnp.bfloat16),
        pltpu.VMEM((cols, 2 * nvec, tile), jnp.bfloat16),
        pltpu.VMEM((tiles, 2 * nvec, tile), jnp.float32),
    ]


def cost(pairs, tile):
    return pl.CostEstimate(flops=int(pairs * tile * tile * 2048), bytes_accessed=4 << 20, transcendentals=0)


def in_smem():
    return pl.BlockSpec(memory_space=pltpu.SMEM)


def in_vmem():
    return pl.BlockSpec(memory_space=pltpu.VMEM)


def own_pairs(ids, packed, feat):
    tiles, width, tile = packed.shape
    nvec = width - feat
    return pl.pallas_call(
        functools.partial(own_kernel, feat),
        out_shape=(
            jax.ShapeDtypeStruct((tiles, 4 * feat, tile), jnp.bfloat16),
            jax.ShapeDtypeStruct((tiles, nvec, tile), jnp.float32),
        ),
        in_specs=[in_smem(), in_vmem()],
        out_specs=(in_vmem(), in_vmem()),
        scratch_shapes=scratch(tiles, feat, nvec, tiles, tile),
        compiler_params=pltpu.CompilerParams(vmem_limit_bytes=LIMIT),
        cost_estimate=cost(8, tile),
        name="own_pairs",
    )(ids, packed)


def mid_pairs(ids, prior, following, near, rows, before, feat):
    tiles, width, tile = prior.shape
    nvec = width - feat
    return pl.pallas_call(
        functools.partial(mid_kernel, feat),
        out_shape=jax.ShapeDtypeStruct((tiles, nvec, tile), jnp.float32),
        in_specs=[in_smem()] + [in_vmem()] * 5,
        out_specs=in_vmem(),
        scratch_shapes=scratch(3 * tiles, feat, nvec, tiles, tile),
        compiler_params=pltpu.CompilerParams(vmem_limit_bytes=LIMIT),
        cost_estimate=cost(18, tile),
        name="mid_pairs",
    )(ids, prior, following, near, rows, before)


def far_pairs(ids, far, rows, before, residual, direction, feat):
    tiles, width, tile = far.shape
    nvec = width - feat
    return pl.pallas_call(
        functools.partial(far_kernel, feat),
        out_shape=(
            jax.ShapeDtypeStruct((tiles, nvec, tile), jnp.float32),
            jax.ShapeDtypeStruct((nvec, 128), jnp.float32),
        ),
        in_specs=[in_smem()] + [in_vmem()] * 5,
        out_specs=(in_vmem(), in_vmem()),
        scratch_shapes=scratch(tiles, feat, nvec, tiles, tile),
        compiler_params=pltpu.CompilerParams(vmem_limit_bytes=LIMIT),
        cost_estimate=cost(6, tile),
        name="far_pairs",
    )(ids, far, rows, before, residual, direction)


def updated(factors, part, *state):
    shape = jax.ShapeDtypeStruct(part.shape, jnp.float32)
    return pl.pallas_call(
        update_kernel,
        out_shape=(shape, shape, shape),
        in_specs=[in_vmem()] * 5,
        out_specs=(in_vmem(), in_vmem(), in_vmem()),
        compiler_params=pltpu.CompilerParams(vmem_limit_bytes=LIMIT),
        name="updated",
    )(factors, part, *state)


def sums_kernel(sums_ref, out_ref, held_ref, blk_ref, grp_ref, send_sem, blk_sem, grp_sem):
    blk_count, grp_count = lax.axis_size("blk"), lax.axis_size("grp")
    blk_index, grp_index = lax.axis_index("blk"), lax.axis_index("grp")
    barrier = pltpu.get_barrier_semaphore()

    def blk_partner(k):
        return (lax.rem(blk_index + k, blk_count), grp_index)

    def grp_partner(k):
        return (blk_index, lax.rem(grp_index + k, grp_count))

    def greet(partner, k, _):
        pl.semaphore_signal(barrier, inc=1, device_id=partner(k), device_id_type=MESH)
        return 0

    lax.fori_loop(1, blk_count, functools.partial(greet, blk_partner), 0)
    lax.fori_loop(1, grp_count, functools.partial(greet, grp_partner), 0)

    held_ref[0] = sums_ref[...]
    pl.semaphore_wait(barrier, blk_count + grp_count - 2)

    def swap(source, landing, sems, partner, count):
        def copy_of(k):
            return pltpu.make_async_remote_copy(
                src_ref=source,
                dst_ref=landing.at[k],
                send_sem=send_sem.at[k],
                recv_sem=sems.at[k],
                device_id=partner(k),
                device_id_type=MESH,
            )

        def begin(k, _):
            copy_of(k).start()
            return 0

        def end(k, _):
            copy_of(k).wait()
            return 0

        lax.fori_loop(1, count, begin, 0)
        lax.fori_loop(1, count, end, 0)

        def add(k, total):
            return total + landing[k]

        return lax.fori_loop(1, count, add, source[...])

    held_ref[1] = swap(held_ref.at[0], blk_ref, blk_sem, blk_partner, blk_count)
    sums = swap(held_ref.at[1], grp_ref, grp_sem, grp_partner, grp_count)
    start_norm, curvature, crossed, length = (sums[:, k : k + 1] for k in range(4))
    step = start_norm / curvature
    fresh_norm = jnp.maximum(start_norm + step * (step * length - 2.0 * crossed), 0.0)
    lane = lax.broadcasted_iota(jnp.int32, sums.shape, 1)
    out_ref[...] = jnp.where(lane == 0, step, fresh_norm / start_norm)


def summed(sums):
    nvec = sums.shape[0]
    blk_count, grp_count = lax.axis_size("blk"), lax.axis_size("grp")
    return pl.pallas_call(
        sums_kernel,
        out_shape=jax.ShapeDtypeStruct((nvec, 128), jnp.float32),
        in_specs=[in_vmem()],
        out_specs=in_vmem(),
        scratch_shapes=[
            pltpu.VMEM((2, nvec, 128), jnp.float32),
            pltpu.VMEM((blk_count, nvec, 128), jnp.float32),
            pltpu.VMEM((grp_count, nvec, 128), jnp.float32),
            pltpu.SemaphoreType.DMA((max(blk_count, grp_count),)),
            pltpu.SemaphoreType.DMA((blk_count,)),
            pltpu.SemaphoreType.DMA((grp_count,)),
        ],
        compiler_params=pltpu.CompilerParams(collective_id=0, has_side_effects=True),
        name="sums",
    )(sums)


def per_device(features, inv_scale, solution, residual, direction, neighbours):
    feat = features.shape[3]
    blk_count, grp_count = lax.axis_size("blk"), lax.axis_size("grp")
    packed = jnp.concatenate([features[0, 0] * inv_scale[:, None], direction[0, 0]], axis=1)
    ids = neighbours[0, 0]
    up = [(i, (i + 1) % blk_count) for i in range(blk_count)]
    down = [((i + 1) % blk_count, i) for i in range(blk_count)]
    swapped = [(i, i + 1 - 2 * (i % 2)) for i in range(grp_count)]
    handed = [(i, i + 2) for i in range(0, grp_count - 2, 2)] + [(i, i - 2) for i in range(3, grp_count, 2)]
    near = lax.ppermute(packed, "grp", swapped)
    prior_blk = lax.ppermute(packed, "blk", up)
    next_blk = lax.ppermute(packed, "blk", down)
    rows, part = own_pairs(ids, packed, feat)
    near, part = lax.optimization_barrier((near, part))
    far = lax.ppermute(near, "grp", handed)
    part = mid_pairs(ids, prior_blk, next_blk, near, rows, part, feat)
    part, sums = far_pairs(ids, far, rows, part, residual[0, 0], direction[0, 0], feat)
    factors = summed(sums)
    outs = updated(factors, part, solution[0, 0], residual[0, 0], direction[0, 0])
    return tuple(out[None, None] for out in outs)


def solution(mesh):
    split = P("blk", "grp", None, None, None)
    in_specs = (split, P(), split, split, split, P("blk", "grp", None, None))
    return jax.shard_map(per_device, mesh=mesh, in_specs=in_specs, out_specs=(split, split, split), check_vma=False)
```
